32 devices in a mesh: groups: 2 (over y), frames: 4 (over z), rows: 4 (over x, core).
Axes of the slice: x: 2, y: 2, z: 4, core: 2. Of those that a mesh axis runs over, the one named last changes fastest.
Arguments:
- latents: bfloat16 [16, 8, 16, 1280], P('rows', ('groups', 'frames')), parts along dimension 1, may hold values from -6 to 6
- spatial_weight: bfloat16 [3, 3, 1280, 1280], P(None, None, None, 'rows'), may hold values from -0.0546875 to 0.0546875
- spatial_bias: float32 [1280], P('rows'), may hold values from -3 to 3
- norm_gain: float32 [1280], P('rows'), may hold values from 0.1 to 1.9
- norm_shift: float32 [1280], P('rows'), may hold values from -3 to 3
- temporal_weight: bfloat16 [3, 1280, 1280], P(None, 'rows'), may hold values from -0.09375 to 0.09375
- temporal_bias: float32 [1280], replicated, may hold values from -3 to 3
- token_gain: float32 [1280], replicated, may hold values from 0.1 to 1.9
- query_weight: bfloat16 [1280, 1024], P(None, 'rows'), may hold values from -4 to 4
- key_weight: bfloat16 [1280, 1024], P(None, 'rows'), may hold values from -4 to 4
- value_weight: bfloat16 [1280, 1024], P(None, 'rows'), may hold values from -0.15625 to 0.15625
- output_weight: bfloat16 [1024, 1280], P('rows'), may hold values from -0.1875 to 0.1875
Outputs:
- denoised: bfloat16 [16, 8, 16, 1280], P('rows', ('groups', 'frames')), parts along dimension 1
The draws below stay inside these ranges and needn't reach their ends.
There are 2 independent parts, one for each index of `groups`. The reference program is written for one: setup_inputs(seed, part) draws one part's arguments, and reference() takes and returns one part's arrays. A program takes and returns all parts, laid end to end along the dimension named above; an argument that names none is the same for every part. Nothing has to cross between parts.
All inputs are finite; a program needn't handle non-finite values.
Results may differ from the reference program's by a relative error of at most 0.034.
Values may be sent and summed in bfloat16 or wider, within the bound.
No kernel may reach another device: no remote copies, remote signals or barrier semaphores. Data moves between devices by JAX's collectives and lax.ppermute only.
A program may use at most 128 MiB of HBM per device.

```python
import math
import jax
import jax.numpy as jnp
from jax import lax

C = 1280
HEADS = 16
HD = 64
NORM_GROUPS = 32
LAT_H = 16
LAT_W = 16
FRAMES = 4
TOKENS = 1024


def shared_basis(key):
    base = jax.random.normal(jax.random.fold_in(key, 101), (C, HEADS * HD), jnp.float32)
    return jnp.clip(base, -5.0, 5.0) / math.sqrt(C)


def own_part(key, salt):
    noise = jax.random.normal(jax.random.fold_in(key, salt), (C, HEADS * HD), jnp.float32)
    return jnp.clip(noise, -5.0, 5.0) / math.sqrt(C)


def draw_query_weight(key, part):
    mixed = 0.6 * shared_basis(key) + 0.8 * own_part(key, 102)
    return jnp.clip(mixed, -4.0, 4.0).astype(jnp.bfloat16)


def draw_key_weight(key, part):
    mixed = 0.6 * shared_basis(key) + 0.8 * own_part(key, 103)
    return jnp.clip(mixed, -4.0, 4.0).astype(jnp.bfloat16)


def shard_levels(rng, dims, pieces, smallest, high):
    loudness, own = 1.0, jax.random.fold_in(rng, 6)
    for dim, shards_of in pieces:
        steps = jnp.exp(jax.random.uniform(jax.random.fold_in(own, dim), (shards_of,), jnp.float32, smallest / len(pieces), high / len(pieces)))
        loudness = loudness * jnp.repeat(steps, dims[dim] // shards_of).reshape([-1 if axis == dim else 1 for axis in range(len(dims))])
    return loudness


def normal_values(rng, shape, width, most, shards=(), kind=jnp.bfloat16):
    entries = width * jax.random.normal(rng, shape, jnp.float32)
    if shards:
        entries = entries * shard_levels(rng, shape, shards, -0.22, 0.18)
    return jnp.clip(entries, -most, most).astype(kind)


def setup_inputs(seed: int = 0, part: int = 0) -> dict:
    splits = jax.random.split(jax.random.key(seed), 13)
    part_splits = jax.random.split(jax.random.fold_in(splits[12], part), 13)
    return {
        "latents": normal_values(part_splits[0], (LAT_H, FRAMES, LAT_W, C), 1.0, 6.0, ((0, 4), (1, 4))),
        "spatial_weight": normal_values(splits[1], (3, 3, C, C), (9 * C) ** -0.5, 0.0546875, ((3, 4),)),
        "spatial_bias": normal_values(splits[2], (C,), 0.5, 3.0, ((0, 4),), jnp.float32),
        "norm_gain": jnp.clip(1.0 + 0.18 * jax.random.normal(splits[3], (C,), jnp.float32), 0.1, 1.9),
        "norm_shift": normal_values(splits[4], (C,), 0.5, 3.0, ((0, 4),), jnp.float32),
        "temporal_weight": normal_values(splits[5], (3, C, C), (3 * C) ** -0.5, 0.09375, ((1, 4),)),
        "temporal_bias": normal_values(splits[6], (C,), 0.5, 3.0, (), jnp.float32),
        "token_gain": jnp.clip(1.0 + 0.18 * jax.random.normal(splits[7], (C,), jnp.float32), 0.1, 1.9),
        "query_weight": draw_query_weight(jax.random.fold_in(splits[12], 71), part),
        "key_weight": draw_key_weight(jax.random.fold_in(splits[12], 71), part),
        "value_weight": normal_values(splits[10], (C, HEADS * HD), C ** -0.5, 0.15625, ((1, 4),)),
        "output_weight": normal_values(splits[11], (HEADS * HD, C), (HEADS * HD) ** -0.5, 0.1875, ((0, 4),)),
    }


def conv_plane(field, weight, bias):
    rows_n, frames_n, cols_n, chans = field.shape
    padded = jnp.pad(field, ((1, 1), (0, 0), (1, 1), (0, 0)))
    total = jnp.zeros((rows_n * frames_n * cols_n, weight.shape[3]), jnp.float32)
    for row_off in range(3):
        for col_off in range(3):
            window = padded[row_off:row_off + rows_n, :, col_off:col_off + cols_n, :].reshape(-1, chans)
            total = total + jnp.dot(window, weight[row_off, col_off], preferred_element_type=jnp.float32)
    return total.reshape(rows_n, frames_n, cols_n, -1) + bias

def head_attention(query, keys, values):
    block = math.gcd(query.shape[0], 1024)
    scale = 1.0 / math.sqrt(HD)

    def one_block(query_block):
        scores = jnp.dot(query_block, keys.T, preferred_element_type=jnp.float32) * scale
        peak = lax.optimization_barrier(jnp.max(scores, axis=-1, keepdims=True))
        weights = jnp.exp(scores - peak)
        denominator = lax.optimization_barrier(jnp.sum(weights, axis=-1, keepdims=True))
        return jnp.dot(weights.astype(jnp.bfloat16), values, preferred_element_type=jnp.float32) / denominator
    return lax.map(one_block, query.reshape(-1, block, HD)).reshape(-1, HD)

def reference(latents, spatial_weight, spatial_bias, norm_gain, norm_shift, temporal_weight, temporal_bias, token_gain, query_weight, key_weight, value_weight, output_weight):
    spatial = conv_plane(latents, spatial_weight, spatial_bias)
    grouped = spatial.reshape(LAT_H, FRAMES, LAT_W, NORM_GROUPS, -1)
    group_mean = lax.optimization_barrier(jnp.mean(grouped, axis=(0, 2, 4), keepdims=True))
    centred = grouped - group_mean
    group_var = lax.optimization_barrier(jnp.mean(centred * centred, axis=(0, 2, 4), keepdims=True))
    scaled = (centred / jnp.sqrt(group_var + 1e-05)).reshape(LAT_H, FRAMES, LAT_W, C) * norm_gain + norm_shift
    activated = jax.nn.silu(scaled).astype(jnp.bfloat16)
    rim = jnp.pad(activated, ((0, 0), (1, 1), (0, 0), (0, 0)))
    temporal = jnp.zeros((LAT_H * FRAMES * LAT_W, C), jnp.float32)
    for lag_index in range(3):
        window = rim[:, lag_index:lag_index + FRAMES].reshape(-1, C)
        temporal = temporal + jnp.dot(window, temporal_weight[lag_index], preferred_element_type=jnp.float32)
    temporal = temporal.reshape(LAT_H, FRAMES, LAT_W, C) + temporal_bias
    hidden = (latents.astype(jnp.float32) + temporal).astype(jnp.bfloat16)
    flat = hidden.reshape(-1, C).astype(jnp.float32)
    token_mean = lax.optimization_barrier(jnp.mean(flat, axis=-1, keepdims=True))
    shifted = flat - token_mean
    token_var = lax.optimization_barrier(jnp.mean(shifted * shifted, axis=-1, keepdims=True))
    normed = (shifted / jnp.sqrt(token_var + 1e-05) * token_gain).astype(jnp.bfloat16)
    queries = jnp.dot(normed, query_weight, preferred_element_type=jnp.float32).astype(jnp.bfloat16)
    keys = jnp.dot(normed, key_weight, preferred_element_type=jnp.float32).astype(jnp.bfloat16)
    values = jnp.dot(normed, value_weight, preferred_element_type=jnp.float32).astype(jnp.bfloat16)

    def by_head(array):
        return array.reshape(TOKENS, HEADS, HD).transpose(1, 0, 2)
    per_head = lax.map(lambda trio: head_attention(trio[0], trio[1], trio[2]), (by_head(queries), by_head(keys), by_head(values)))
    attended = per_head.transpose(1, 0, 2).reshape(TOKENS, HEADS * HD).astype(jnp.bfloat16)
    projected = jnp.dot(attended, output_weight, preferred_element_type=jnp.float32)
    denoised = hidden.reshape(-1, C).astype(jnp.float32) + projected
    return denoised.reshape(LAT_H, FRAMES, LAT_W, C).astype(jnp.bfloat16)
```

```python
import functools
import math

import jax
import jax.numpy as jnp
from jax import lax
from jax.experimental import pallas as pl
from jax.experimental.pallas import tpu as pltpu
from jax.sharding import PartitionSpec as P

HD = 64
NORM_GROUPS = 32
VMEM_LIMIT = 16 * 1024 * 1024


def swap(array, axis, stride):
    size = lax.axis_size(axis)
    return lax.ppermute(array, axis, [(i, i ^ stride) for i in range(size)])


def neighbours(array, axis):
    size = lax.axis_size(axis)
    even = [(i, i ^ 1) for i in range(size) if i ^ 1 < size]
    odd = [(i, ((i + 1) ^ 1) - 1) for i in range(1, size) if ((i + 1) ^ 1) - 1 < size]
    return lax.ppermute(array, axis, even), lax.ppermute(array, axis, odd)


def load_kernel(*refs):
    half = len(refs) // 2
    sems = refs[-1]
    copies = [
        pltpu.make_async_copy(source, target, sems.at[i])
        for i, (source, target) in enumerate(zip(refs[:half], refs[half : 2 * half]))
    ]
    for copy in copies:
        copy.start()
    for copy in copies:
        copy.wait()


def load(*arrays):
    return pl.pallas_call(
        load_kernel,
        out_shape=[jax.ShapeDtypeStruct(a.shape, a.dtype) for a in arrays],
        in_specs=[pl.BlockSpec(memory_space=pltpu.HBM)] * len(arrays),
        out_specs=[pl.BlockSpec(memory_space=pltpu.VMEM)] * len(arrays),
        scratch_shapes=[pltpu.SemaphoreType.DMA((len(arrays),))],
        compiler_params=pltpu.CompilerParams(vmem_limit_bytes=VMEM_LIMIT),
        cost_estimate=pl.CostEstimate(
            flops=0, bytes_accessed=sum(a.size * a.dtype.itemsize for a in arrays), transcendentals=0
        ),
    )(*arrays)


def conv_kernel(*refs, pieces, cols, groups, axis):
    plane_refs = refs[:pieces]
    weight_ref, bias_ref, gain_ref, shift_ref, out_ref, padded_ref = refs[pieces:]
    share, chans = plane_refs[0].shape
    tokens = pieces * share
    outs = out_ref.shape[0]
    padded_ref[0:cols] = jnp.zeros((cols, chans), padded_ref.dtype)
    padded_ref[cols + tokens : tokens + 2 * cols] = jnp.zeros((cols, chans), padded_ref.dtype)
    index = lax.axis_index(axis)
    for mask, piece in enumerate(plane_refs):
        start = pl.multiple_of((index ^ mask) * share + cols, math.gcd(share, cols))
        padded_ref[pl.ds(start, share)] = piece[...]
    total = None
    for row_off in range(3):
        window = padded_ref[row_off * cols : row_off * cols + tokens]
        weight = weight_ref[row_off].reshape(3 * outs, chans)
        term = lax.dot_general(
            weight, window, (((1,), (1,)), ((), ())), preferred_element_type=jnp.float32
        )
        total = term if total is None else total + term
    column = lax.broadcasted_iota(jnp.int32, (outs, tokens), 1) % cols
    left = jnp.where(column == 0, 0.0, pltpu.roll(total[:outs], 1, 1))
    right = jnp.where(column == cols - 1, 0.0, pltpu.roll(total[2 * outs :], tokens - 1, 1))

    diagonal = lax.broadcasted_iota(jnp.int32, (outs, outs), 0) == lax.broadcasted_iota(
        jnp.int32, (outs, outs), 1
    )

    def upright(row):
        return jnp.sum(jnp.where(diagonal, row[None], 0.0), axis=1, keepdims=True)

    spatial = total[outs : 2 * outs] + left + right + upright(bias_ref[...])
    per_group = outs // groups
    count = per_group * tokens

    def group_mean(values):
        sums = jnp.sum(values, axis=1, keepdims=True).reshape(groups, per_group, 1)
        sums = jnp.sum(sums, axis=1, keepdims=True) * (1.0 / count)
        return jnp.broadcast_to(sums, (groups, per_group, 1)).reshape(outs, 1)

    centred = spatial - group_mean(spatial)
    inverse = 1.0 / jnp.sqrt(group_mean(centred * centred) + 1e-05)
    scaled = centred * (inverse * upright(gain_ref[...])) + upright(shift_ref[...])
    out_ref[...] = (scaled / (1.0 + jnp.exp(-scaled))).astype(out_ref.dtype)


def conv_norm(pieces, weight, bias, gain, shift, cols, groups, rows_axis):
    share, chans = pieces[0].shape
    tokens, outs = share * len(pieces), weight.shape[2]
    return pl.pallas_call(
        functools.partial(
            conv_kernel, pieces=len(pieces), cols=cols, groups=groups, axis=rows_axis
        ),
        out_shape=jax.ShapeDtypeStruct((outs, tokens), jnp.bfloat16),
        in_specs=[pl.BlockSpec(memory_space=pltpu.VMEM)] * (len(pieces) + 4),
        out_specs=pl.BlockSpec(memory_space=pltpu.VMEM),
        scratch_shapes=[pltpu.VMEM((tokens + 2 * cols, chans), jnp.bfloat16)],
        compiler_params=pltpu.CompilerParams(vmem_limit_bytes=VMEM_LIMIT),
        cost_estimate=pl.CostEstimate(
            flops=18 * tokens * outs * chans,
            bytes_accessed=2 * (weight.size + tokens * chans + outs * tokens),
            transcendentals=outs * tokens,
        ),
    )(*pieces, weight, bias, gain, shift)


def spread_kernel(*refs, places, frames_axis, rows_axis):
    pieces = refs[: len(places)]
    weight_ref, send_ref, keep_ref, stack_ref, total_ref = refs[len(places) :]
    k = pieces[0].shape[0]
    inner_count, outer_count, width, _ = total_ref.shape
    is_odd = lax.rem(lax.axis_index(frames_axis), 2)
    for piece, (even, odd) in zip(pieces, places):
        start = even * k if even == odd else pl.multiple_of((even + is_odd * (odd - even)) * k, 16)
        stack_ref[pl.ds(start, k)] = piece[...]
    total = lax.dot_general(
        stack_ref[...],
        weight_ref[...],
        (((0,), (0,)), ((), ())),
        preferred_element_type=jnp.float32,
    )
    for outer in range(outer_count):
        for inner in range(inner_count):
            start = (outer * inner_count + inner) * width
            total_ref[inner, outer] = total[start : start + width]
    mine = lax.rem(lax.axis_index(rows_axis), inner_count)
    send_ref[...] = total_ref[1 - mine].astype(send_ref.dtype)
    keep_ref[...] = total_ref[mine]


def spread(pieces, places, weight, outer_count, frames_axis, rows_axis):
    k, tokens = pieces[0].shape
    channels = weight.shape[1]
    part = (outer_count, tokens // (2 * outer_count), channels)
    return pl.pallas_call(
        functools.partial(
            spread_kernel, places=places, frames_axis=frames_axis, rows_axis=rows_axis
        ),
        out_shape=[
            jax.ShapeDtypeStruct(part, jnp.bfloat16),
            jax.ShapeDtypeStruct(part, jnp.float32),
        ],
        in_specs=[pl.BlockSpec(memory_space=pltpu.VMEM)] * (len(pieces) + 1),
        out_specs=[pl.BlockSpec(memory_space=pltpu.VMEM)] * 2,
        scratch_shapes=[
            pltpu.VMEM((len(pieces) * k, tokens), jnp.bfloat16),
            pltpu.VMEM((2,) + part, jnp.float32),
        ],
        compiler_params=pltpu.CompilerParams(vmem_limit_bytes=VMEM_LIMIT),
        cost_estimate=pl.CostEstimate(
            flops=2 * len(pieces) * tokens * k * channels,
            bytes_accessed=2 * weight.size + 6 * tokens * channels,
            transcendentals=0,
        ),
    )(*pieces, weight)


def merge_kernel(mine_ref, theirs_ref, *refs, axis, inner_count):
    place = lax.div(lax.axis_index(axis), inner_count)
    for mask, (send_ref, keep_ref) in enumerate(zip(refs[::2], refs[1::2])):
        total = mine_ref[place ^ mask] + theirs_ref[place ^ mask].astype(jnp.float32)
        send_ref[...] = total.astype(send_ref.dtype)
        keep_ref[...] = total


def merge(mine, theirs, rows_axis, inner_count):
    shapes = [
        jax.ShapeDtypeStruct(theirs.shape[1:], dtype) for dtype in (jnp.bfloat16, jnp.float32)
    ] * theirs.shape[0]
    outs = pl.pallas_call(
        functools.partial(merge_kernel, axis=rows_axis, inner_count=inner_count),
        out_shape=shapes,
        in_specs=[pl.BlockSpec(memory_space=pltpu.VMEM)] * 2,
        out_specs=[pl.BlockSpec(memory_space=pltpu.VMEM)] * len(shapes),
        compiler_params=pltpu.CompilerParams(vmem_limit_bytes=VMEM_LIMIT),
        cost_estimate=pl.CostEstimate(
            flops=theirs.size, bytes_accessed=12 * theirs.size, transcendentals=0
        ),
    )(mine, theirs)
    return outs[::2], outs[1::2]


def deal_kernel(own_ref, pair_ref, out_ref, *, frames_axis, rows_axis, inner_count):
    _, rows, width, _ = out_ref.shape
    is_odd = lax.rem(lax.axis_index(frames_axis), 2)
    index = lax.axis_index(rows_axis)
    for source, frame in ((own_ref, is_odd), (pair_ref, 1 - is_odd)):
        for mask in range(rows):
            place = mask // inner_count * inner_count + lax.rem(index ^ mask, inner_count)
            start = pl.multiple_of(place * width, width)
            out_ref[frame, index ^ mask] = source[pl.ds(start, width)]


def deal(own, pair, rows, frames_axis, rows_axis, inner_count):
    tokens, columns = own.shape
    return pl.pallas_call(
        functools.partial(
            deal_kernel, frames_axis=frames_axis, rows_axis=rows_axis, inner_count=inner_count
        ),
        out_shape=jax.ShapeDtypeStruct((2, rows, tokens // rows, columns), jnp.bfloat16),
        in_specs=[pl.BlockSpec(memory_space=pltpu.VMEM)] * 2,
        out_specs=pl.BlockSpec(memory_space=pltpu.VMEM),
        compiler_params=pltpu.CompilerParams(vmem_limit_bytes=VMEM_LIMIT),
        cost_estimate=pl.CostEstimate(
            flops=0, bytes_accessed=8 * tokens * columns, transcendentals=0
        ),
    )(own, pair)


def finish_kernel(attended_ref, *refs, axis):
    weights, (hidden_ref, out_ref) = refs[:-2], refs[-2:]
    index = lax.axis_index(axis)
    total = hidden_ref[...].astype(jnp.float32)
    for mask, weight in enumerate(weights):
        halves = [attended_ref[frame, index ^ mask] for frame in range(2)]
        columns = jnp.concatenate(halves, axis=1)
        total = total + jnp.dot(columns, weight[...], preferred_element_type=jnp.float32)
    out_ref[...] = total.astype(out_ref.dtype)


def finish(attended, weights, hidden, rows_axis):
    return pl.pallas_call(
        functools.partial(finish_kernel, axis=rows_axis),
        out_shape=jax.ShapeDtypeStruct(hidden.shape, hidden.dtype),
        in_specs=[pl.BlockSpec(memory_space=pltpu.VMEM)] * (len(weights) + 2),
        out_specs=pl.BlockSpec(memory_space=pltpu.VMEM),
        compiler_params=pltpu.CompilerParams(vmem_limit_bytes=VMEM_LIMIT),
        cost_estimate=pl.CostEstimate(
            flops=2 * hidden.shape[0] * len(weights) * weights[0].size,
            bytes_accessed=2 * len(weights) * weights[0].size + 4 * hidden.size,
            transcendentals=0,
        ),
    )(attended, *weights, hidden)


def norm_kernel(latents_ref, mine_ref, theirs_ref, bias_ref, gain_ref, normed_ref, *hidden_refs):
    temporal = mine_ref[...] + theirs_ref[...].astype(jnp.float32) + bias_ref[...][None]
    hidden = latents_ref[...].astype(jnp.float32) + temporal
    hidden = hidden.astype(normed_ref.dtype)
    for hidden_ref in hidden_refs:
        hidden_ref[...] = hidden
    flat = hidden.astype(jnp.float32)
    scale = 1.0 / flat.shape[-1]
    shifted = flat - jnp.sum(flat, axis=-1, keepdims=True) * scale
    variance = jnp.sum(shifted * shifted, axis=-1, keepdims=True) * scale
    normed = shifted * (1.0 / jnp.sqrt(variance + 1e-05)) * gain_ref[...][None]
    normed_ref[...] = normed.astype(normed_ref.dtype)


def norm_of_hidden(latents, mine, theirs, bias, gain, with_hidden):
    shapes = [jax.ShapeDtypeStruct(theirs.shape, jnp.bfloat16)] * (2 if with_hidden else 1)
    return pl.pallas_call(
        norm_kernel,
        out_shape=shapes,
        in_specs=[pl.BlockSpec(memory_space=pltpu.VMEM)] * 5,
        out_specs=[pl.BlockSpec(memory_space=pltpu.VMEM)] * len(shapes),
        compiler_params=pltpu.CompilerParams(vmem_limit_bytes=VMEM_LIMIT),
        cost_estimate=pl.CostEstimate(
            flops=12 * theirs.size, bytes_accessed=12 * theirs.size, transcendentals=0
        ),
    )(latents, mine, theirs, bias, gain)


def project_kernel(*refs, pieces, frames_axis, rows_axis):
    q_ref, k_ref, v_ref, own_q, own_kv, pair_qkv, pair_kv, flat_ref, scratch = refs[pieces:]
    index = lax.axis_index(rows_axis)
    for mask, piece in enumerate(refs[:pieces]):
        flat_ref[lax.rem(index ^ mask, pieces)] = piece[...]
    flat = flat_ref[...].reshape(-1, flat_ref.shape[-1])
    _, _, share, _, tokens = scratch.shape
    for which, weight_ref in enumerate((q_ref, k_ref, v_ref)):
        product = jnp.dot(flat, weight_ref[...], preferred_element_type=jnp.float32)
        upright = product.T.astype(scratch.dtype)
        scratch[:, which] = upright.reshape(2, share, HD, tokens)
    is_odd = lax.rem(lax.axis_index(frames_axis), 2)
    own_q[...] = scratch[is_odd, 0]
    own_kv[...] = scratch[is_odd, 1:]
    pair_qkv[...] = scratch[1 - is_odd]
    pair_kv[...] = scratch[1 - is_odd, 1:]


def project(pieces, query_weight, key_weight, value_weight, frames_axis, rows_axis):
    width, channels = pieces[0].shape
    tokens = len(pieces) * width
    share = query_weight.shape[1] // HD // 2

    def shape(count):
        return jax.ShapeDtypeStruct((count, share, HD, tokens), jnp.bfloat16)

    return pl.pallas_call(
        functools.partial(
            project_kernel, pieces=len(pieces), frames_axis=frames_axis, rows_axis=rows_axis
        ),
        out_shape=[
            jax.ShapeDtypeStruct((share, HD, tokens), jnp.bfloat16),
            shape(2),
            shape(3),
            shape(2),
        ],
        in_specs=[pl.BlockSpec(memory_space=pltpu.VMEM)] * (len(pieces) + 3),
        out_specs=[pl.BlockSpec(memory_space=pltpu.VMEM)] * 4,
        scratch_shapes=[
            pltpu.VMEM((len(pieces), width, channels), jnp.bfloat16),
            pltpu.VMEM((2, 3, share, HD, tokens), jnp.bfloat16),
        ],
        compiler_params=pltpu.CompilerParams(vmem_limit_bytes=VMEM_LIMIT),
        cost_estimate=pl.CostEstimate(
            flops=6 * tokens * channels * query_weight.shape[1],
            bytes_accessed=6 * query_weight.size + 2 * tokens * channels,
            transcendentals=0,
        ),
    )(*pieces, query_weight, key_weight, value_weight)


def attention_kernel(*refs, parts, kv_count, first, last):
    own_q, kvs = refs[:parts], refs[parts : parts + kv_count]
    rest = refs[parts + kv_count :]
    pair_qkv, rest = rest[:parts], rest[parts:]
    state, outs = ((), rest) if first else (rest[:3], rest[3:])
    scale = 1.0 / math.sqrt(HD)
    contract_first = (((0,), (0,)), ((), ()))

    def wide(arrays):
        return jnp.concatenate(list(arrays), axis=1)

    for head in range(own_q[0].shape[0]):
        pairs = [(kv[0, head], kv[1, head]) for kv in kvs]
        if first:
            pairs += [(qkv[1, head], qkv[2, head]) for qkv in pair_qkv]
        groups = [pairs[i : i + parts] for i in range(0, len(pairs), parts)]
        keys = [wide(key for key, _ in group) for group in groups]
        values = [wide(value for _, value in group) for group in groups]
        asked = (wide(q[head] for q in own_q), wide(qkv[0, head] for qkv in pair_qkv))
        for which, query in enumerate(asked):
            query = (query.astype(jnp.float32) * scale).astype(jnp.bfloat16)
            scores = [
                lax.dot_general(key, query, contract_first, preferred_element_type=jnp.float32)
                for key in keys
            ]
            peak = functools.reduce(
                jnp.maximum, [jnp.max(s, axis=0, keepdims=True) for s in scores]
            )
            if first:
                denominator = jnp.zeros_like(peak)
                numerator = jnp.zeros((HD, query.shape[1]), jnp.float32)
            else:
                old_peak, denominator, numerator = (ref[head, which] for ref in state)
                peak = jnp.maximum(peak, old_peak)
                shrink = jnp.exp(old_peak - peak)
                denominator, numerator = denominator * shrink, numerator * shrink
            for value, score in zip(values, scores):
                weights = jnp.exp(score - peak)
                denominator = denominator + jnp.sum(weights, axis=0, keepdims=True)
                numerator = numerator + jnp.dot(
                    value, weights.astype(jnp.bfloat16), preferred_element_type=jnp.float32
                )
            if last:
                out = outs[which]
                result = (numerator / denominator).T
                out[:, head * HD : (head + 1) * HD] = result.astype(out.dtype)
            else:
                for ref, value in zip(outs, (peak, denominator, numerator)):
                    ref[head, which] = value


def attend(own_q, pair_qkv, kvs, state, last):
    parts = len(own_q)
    heads, _, width = own_q[0].shape
    tokens = parts * width
    keys = (len(kvs) + (0 if state else parts)) * width
    if last:
        shapes = [jax.ShapeDtypeStruct((tokens, heads * HD), jnp.bfloat16)] * 2
    else:
        shapes = [
            jax.ShapeDtypeStruct((heads, 2, rows, tokens), jnp.float32) for rows in (1, 1, HD)
        ]
    work = 2 * heads * tokens * keys
    args = (*own_q, *kvs, *pair_qkv, *state)
    return pl.pallas_call(
        functools.partial(
            attention_kernel, parts=parts, kv_count=len(kvs), first=not state, last=last
        ),
        out_shape=shapes,
        in_specs=[pl.BlockSpec(memory_space=pltpu.VMEM)] * len(args),
        out_specs=[pl.BlockSpec(memory_space=pltpu.VMEM)] * len(shapes),
        compiler_params=pltpu.CompilerParams(vmem_limit_bytes=VMEM_LIMIT),
        cost_estimate=pl.CostEstimate(
            flops=4 * work * HD,
            bytes_accessed=sum(a.size * a.dtype.itemsize for a in args),
            transcendentals=work,
        ),
    )(*args)


def body(
    latents,
    spatial_weight,
    spatial_bias,
    norm_gain,
    norm_shift,
    temporal_weight,
    temporal_bias,
    token_gain,
    query_weight,
    key_weight,
    value_weight,
    output_weight,
):
    rows_size, frames_size = lax.axis_size("rows"), lax.axis_size("frames")
    row_count, frame_count, width_cells, channels = latents.shape
    if rows_size != 4 or frames_size < 2 or frames_size & (frames_size - 1) or frame_count != 1:
        raise NotImplementedError("mesh shape")
    inner_size = 2
    outer_size = rows_size // inner_size
    loaded = load(jnp.swapaxes(spatial_weight, 2, 3))
    own = latents.reshape(-1, channels)
    pieces = {0: own}
    bit = rows_size // 2
    while bit > 1:
        pieces.update({m | bit: swap(piece, "rows", bit) for m, piece in pieces.items()})
        bit //= 2
    far, loaded, output_weight = lax.optimization_barrier(
        ({m: pieces[m] for m in pieces if m}, loaded, output_weight)
    )
    pieces.update(far)
    weights = {m: swap(output_weight, "rows", m) for m in (inner_size, 1)}
    weights[0] = output_weight
    pieces.update({m | 1: swap(piece, "rows", 1) for m, piece in pieces.items()})
    pieces = [pieces[m] for m in range(rows_size)]
    local_out = spatial_weight.shape[3]
    activated = conv_norm(
        pieces,
        *loaded,
        spatial_bias,
        norm_gain,
        norm_shift,
        width_cells,
        NORM_GROUPS // rows_size,
        "rows",
    )
    first, second = neighbours(activated, "frames")
    send, chip_sum = spread(
        [activated, first, second],
        ((1, 1), (2, 0), (0, 2)),
        temporal_weight.reshape(3 * local_out, channels),
        outer_size,
        "frames",
        "rows",
    )
    sends, keeps = merge(chip_sum, swap(send, "rows", 1), "rows", inner_size)
    sends, weights = lax.optimization_barrier((sends, weights))
    weights[inner_size + 1] = swap(weights[inner_size], "rows", 1)
    others = [swap(sends[1 - mask], "rows", inner_size) for mask in range(outer_size)]
    own_q, own_kv, pair_qkv, far = [], [], [], []
    for mask in range(outer_size):
        latent_rows, other = pieces[mask * inner_size], others[mask]
        if mask:
            other, weights = lax.optimization_barrier((other, weights))
        normed, *wanted = norm_of_hidden(
            latent_rows, keeps[mask], other, temporal_bias, token_gain, mask == 0
        )
        hidden = wanted[0] if wanted else hidden
        q, kv, *sent = project(
            [normed, swap(normed, "rows", 1)],
            query_weight,
            key_weight,
            value_weight,
            "frames",
            "rows",
        )
        own_q.append(q)
        own_kv.append(kv)
        far.append(
            [
                swap(sent[1] if m % 2 else kv, "frames", m)
                for m in range(frames_size - 1, 1, -1)
            ]
        )
        pair_qkv.append(swap(sent[0], "frames", 1))
    early, late = own_kv + far[0][:1], far[0][1:] + far[1]
    state = attend(own_q, pair_qkv, early, (), not late)
    own_out, pair_out = attend(own_q, pair_qkv, late, state, True) if late else state
    dealt = deal(own_out, pair_out, rows_size, "frames", "rows", inner_size)
    together = 2 * rows_size
    groups = [
        list(range(start, start + together))
        for start in range(0, frames_size * rows_size, together)
    ]
    arrived = lax.all_to_all(
        dealt.reshape((together,) + dealt.shape[2:]),
        ("frames", "rows"),
        0,
        0,
        axis_index_groups=groups,
        tiled=True,
    )
    weights = [weights[m] for m in range(rows_size)]
    result = finish(arrived.reshape(dealt.shape), weights, hidden, "rows")
    return result.reshape(latents.shape)


def solution(mesh):
    in_specs = (
        P("rows", ("groups", "frames"), None, None),
        P(None, None, None, "rows"),
        P("rows"),
        P("rows"),
        P("rows"),
        P(None, "rows", None),
        P(),
        P(),
        P(None, "rows"),
        P(None, "rows"),
        P(None, "rows"),
        P("rows", None),
    )
    out_specs = P("rows", ("groups", "frames"), None, None)
    return jax.shard_map(body, mesh=mesh, in_specs=in_specs, out_specs=out_specs, check_vma=False)
```

```python
import functools
import math

import jax
import jax.numpy as jnp
from jax import lax
from jax.experimental import pallas as pl
from jax.experimental.pallas import tpu as pltpu
from jax.sharding import PartitionSpec as P

HD = 64
NORM_GROUPS = 32
VMEM_LIMIT = 16 * 1024 * 1024


def swap(array, axis, stride):
    size = lax.axis_size(axis)
    return lax.ppermute(array, axis, [(i, i ^ stride) for i in range(size)])


def neighbours(array, axis):
    size = lax.axis_size(axis)
    even = [(i, i ^ 1) for i in range(size) if i ^ 1 < size]
    odd = [(i, ((i + 1) ^ 1) - 1) for i in range(1, size) if ((i + 1) ^ 1) - 1 < size]
    return lax.ppermute(array, axis, even), lax.ppermute(array, axis, odd)


def load_kernel(*refs):
    half = len(refs) // 2
    sems = refs[-1]
    copies = [
        pltpu.make_async_copy(source, target, sems.at[i])
        for i, (source, target) in enumerate(zip(refs[:half], refs[half : 2 * half]))
    ]
    for copy in copies:
        copy.start()
    for copy in copies:
        copy.wait()


def load(*arrays):
    return pl.pallas_call(
        load_kernel,
        out_shape=[jax.ShapeDtypeStruct(a.shape, a.dtype) for a in arrays],
        in_specs=[pl.BlockSpec(memory_space=pltpu.HBM)] * len(arrays),
        out_specs=[pl.BlockSpec(memory_space=pltpu.VMEM)] * len(arrays),
        scratch_shapes=[pltpu.SemaphoreType.DMA((len(arrays),))],
        compiler_params=pltpu.CompilerParams(vmem_limit_bytes=VMEM_LIMIT),
        cost_estimate=pl.CostEstimate(
            flops=0, bytes_accessed=sum(a.size * a.dtype.itemsize for a in arrays), transcendentals=0
        ),
    )(*arrays)


def conv_kernel(*refs, pieces, cols, groups, axis):
    plane_refs = refs[:pieces]
    weight_ref, bias_ref, gain_ref, shift_ref, out_ref, padded_ref = refs[pieces:]
    share, chans = plane_refs[0].shape
    tokens = pieces * share
    outs = out_ref.shape[0]
    padded_ref[0:cols] = jnp.zeros((cols, chans), padded_ref.dtype)
    padded_ref[cols + tokens : tokens + 2 * cols] = jnp.zeros((cols, chans), padded_ref.dtype)
    index = lax.axis_index(axis)
    for mask, piece in enumerate(plane_refs):
        start = pl.multiple_of((index ^ mask) * share + cols, math.gcd(share, cols))
        padded_ref[pl.ds(start, share)] = piece[...]
    total = None
    for row_off in range(3):
        window = padded_ref[row_off * cols : row_off * cols + tokens]
        weight = weight_ref[row_off].reshape(3 * outs, chans)
        term = lax.dot_general(
            weight, window, (((1,), (1,)), ((), ())), preferred_element_type=jnp.float32
        )
        total = term if total is None else total + term
    column = lax.broadcasted_iota(jnp.int32, (outs, tokens), 1) % cols
    left = jnp.where(column == 0, 0.0, pltpu.roll(total[:outs], 1, 1))
    right = jnp.where(column == cols - 1, 0.0, pltpu.roll(total[2 * outs :], tokens - 1, 1))

    diagonal = lax.broadcasted_iota(jnp.int32, (outs, outs), 0) == lax.broadcasted_iota(
        jnp.int32, (outs, outs), 1
    )

    def upright(row):
        return jnp.sum(jnp.where(diagonal, row[None], 0.0), axis=1, keepdims=True)

    spatial = total[outs : 2 * outs] + left + right + upright(bias_ref[...])
    per_group = outs // groups
    count = per_group * tokens

    def group_mean(values):
        sums = jnp.sum(values, axis=1, keepdims=True).reshape(groups, per_group, 1)
        sums = jnp.sum(sums, axis=1, keepdims=True) * (1.0 / count)
        return jnp.broadcast_to(sums, (groups, per_group, 1)).reshape(outs, 1)

    centred = spatial - group_mean(spatial)
    inverse = 1.0 / jnp.sqrt(group_mean(centred * centred) + 1e-05)
    scaled = centred * (inverse * upright(gain_ref[...])) + upright(shift_ref[...])
    out_ref[...] = (scaled / (1.0 + jnp.exp(-scaled))).astype(out_ref.dtype)


def conv_norm(pieces, weight, bias, gain, shift, cols, groups, rows_axis):
    share, chans = pieces[0].shape
    tokens, outs = share * len(pieces), weight.shape[2]
    return pl.pallas_call(
        functools.partial(
            conv_kernel, pieces=len(pieces), cols=cols, groups=groups, axis=rows_axis
        ),
        out_shape=jax.ShapeDtypeStruct((outs, tokens), jnp.bfloat16),
        in_specs=[pl.BlockSpec(memory_space=pltpu.VMEM)] * (len(pieces) + 4),
        out_specs=pl.BlockSpec(memory_space=pltpu.VMEM),
        scratch_shapes=[pltpu.VMEM((tokens + 2 * cols, chans), jnp.bfloat16)],
        compiler_params=pltpu.CompilerParams(vmem_limit_bytes=VMEM_LIMIT),
        cost_estimate=pl.CostEstimate(
            flops=18 * tokens * outs * chans,
            bytes_accessed=2 * (weight.size + tokens * chans + outs * tokens),
            transcendentals=outs * tokens,
        ),
    )(*pieces, weight, bias, gain, shift)


def spread_kernel(*refs, places, parity_axes, rows_axis):
    pieces = refs[: len(places)]
    weight_ref, send_ref, rest_ref, stack_ref, rows_ref = refs[len(places) :]
    k = pieces[0].shape[0]
    outer_count, width, _ = rest_ref.shape
    inner_count = rows_ref.shape[0] // outer_count
    is_odd = lax.rem(sum(lax.axis_index(axis) for axis in parity_axes), 2)
    for piece, (even, odd) in zip(pieces, places):
        start = even * k if even == odd else pl.multiple_of((even + is_odd * (odd - even)) * k, 16)
        stack_ref[pl.ds(start, k)] = piece[...]
    rows_ref[...] = stack_ref[...].T.reshape(rows_ref.shape)
    mine = lax.rem(lax.axis_index(rows_axis), inner_count)
    sent = [rows_ref[outer * inner_count + 1 - mine] for outer in range(outer_count)]
    product = jnp.dot(
        jnp.concatenate(sent, axis=0), weight_ref[...], preferred_element_type=jnp.float32
    )
    send_ref[...] = product.astype(send_ref.dtype).reshape(send_ref.shape)
    for outer in range(outer_count):
        rest_ref[outer] = rows_ref[outer * inner_count + mine]


def keep_kernel(rest_ref, weight_ref, keep_ref):
    rest = rest_ref[...].reshape(-1, rest_ref.shape[-1])
    product = jnp.dot(rest, weight_ref[...], preferred_element_type=jnp.float32)
    keep_ref[...] = product.reshape(keep_ref.shape)


def spread(pieces, places, weight, outer_count, parity_axes, rows_axis):
    k, tokens = pieces[0].shape
    depth, channels = weight.shape
    width = tokens // (2 * outer_count)
    part = (outer_count, width, channels)
    estimate = pl.CostEstimate(
        flops=tokens * depth * channels,
        bytes_accessed=2 * weight.size + 3 * tokens * channels,
        transcendentals=0,
    )
    send, rest = pl.pallas_call(
        functools.partial(
            spread_kernel, places=places, parity_axes=parity_axes, rows_axis=rows_axis
        ),
        out_shape=[
            jax.ShapeDtypeStruct(part, jnp.bfloat16),
            jax.ShapeDtypeStruct((outer_count, width, depth), jnp.bfloat16),
        ],
        in_specs=[pl.BlockSpec(memory_space=pltpu.VMEM)] * (len(pieces) + 1),
        out_specs=[pl.BlockSpec(memory_space=pltpu.VMEM)] * 2,
        scratch_shapes=[
            pltpu.VMEM((depth, tokens), jnp.bfloat16),
            pltpu.VMEM((2 * outer_count, width, depth), jnp.bfloat16),
        ],
        compiler_params=pltpu.CompilerParams(vmem_limit_bytes=VMEM_LIMIT),
        cost_estimate=estimate,
    )(*pieces, weight)
    keep = pl.pallas_call(
        keep_kernel,
        out_shape=jax.ShapeDtypeStruct(part, jnp.float32),
        in_specs=[pl.BlockSpec(memory_space=pltpu.VMEM)] * 2,
        out_specs=pl.BlockSpec(memory_space=pltpu.VMEM),
        compiler_params=pltpu.CompilerParams(vmem_limit_bytes=VMEM_LIMIT),
        cost_estimate=estimate,
    )(rest, weight)
    return send, keep


def merge_kernel(mine_ref, theirs_ref, *refs, axis, inner_count):
    place = lax.div(lax.axis_index(axis), inner_count)
    for mask, (send_ref, keep_ref) in enumerate(zip(refs[::2], refs[1::2])):
        total = mine_ref[place ^ mask] + theirs_ref[place ^ mask].astype(jnp.float32)
        send_ref[...] = total.astype(send_ref.dtype)
        keep_ref[...] = total


def merge(mine, theirs, rows_axis, inner_count):
    shapes = [
        jax.ShapeDtypeStruct(theirs.shape[1:], dtype) for dtype in (jnp.bfloat16, jnp.float32)
    ] * theirs.shape[0]
    outs = pl.pallas_call(
        functools.partial(merge_kernel, axis=rows_axis, inner_count=inner_count),
        out_shape=shapes,
        in_specs=[pl.BlockSpec(memory_space=pltpu.VMEM)] * 2,
        out_specs=[pl.BlockSpec(memory_space=pltpu.VMEM)] * len(shapes),
        compiler_params=pltpu.CompilerParams(vmem_limit_bytes=VMEM_LIMIT),
        cost_estimate=pl.CostEstimate(
            flops=theirs.size, bytes_accessed=12 * theirs.size, transcendentals=0
        ),
    )(mine, theirs)
    return outs[::2], outs[1::2]


def deal_kernel(own_ref, pair_ref, out_ref, *, frames_axis, rows_axis, inner_count):
    _, rows, width, _ = out_ref.shape
    is_odd = lax.rem(lax.axis_index(frames_axis), 2)
    index = lax.axis_index(rows_axis)
    for source, frame in ((own_ref, is_odd), (pair_ref, 1 - is_odd)):
        for mask in range(rows):
            place = mask // inner_count * inner_count + lax.rem(index ^ mask, inner_count)
            start = pl.multiple_of(place * width, width)
            out_ref[frame, index ^ mask] = source[pl.ds(start, width)]


def deal(own, pair, rows, frames_axis, rows_axis, inner_count):
    tokens, columns = own.shape
    return pl.pallas_call(
        functools.partial(
            deal_kernel, frames_axis=frames_axis, rows_axis=rows_axis, inner_count=inner_count
        ),
        out_shape=jax.ShapeDtypeStruct((2, rows, tokens // rows, columns), jnp.bfloat16),
        in_specs=[pl.BlockSpec(memory_space=pltpu.VMEM)] * 2,
        out_specs=pl.BlockSpec(memory_space=pltpu.VMEM),
        compiler_params=pltpu.CompilerParams(vmem_limit_bytes=VMEM_LIMIT),
        cost_estimate=pl.CostEstimate(
            flops=0, bytes_accessed=8 * tokens * columns, transcendentals=0
        ),
    )(own, pair)


def finish_kernel(attended_ref, *refs, axis):
    weights, (hidden_ref, out_ref) = refs[:-2], refs[-2:]
    index = lax.axis_index(axis)
    total = hidden_ref[...].astype(jnp.float32)
    for mask, weight in enumerate(weights):
        halves = [attended_ref[frame, index ^ mask] for frame in range(2)]
        columns = jnp.concatenate(halves, axis=1)
        total = total + jnp.dot(columns, weight[...], preferred_element_type=jnp.float32)
    out_ref[...] = total.astype(out_ref.dtype)


def finish(attended, weights, hidden, rows_axis):
    return pl.pallas_call(
        functools.partial(finish_kernel, axis=rows_axis),
        out_shape=jax.ShapeDtypeStruct(hidden.shape, hidden.dtype),
        in_specs=[pl.BlockSpec(memory_space=pltpu.VMEM)] * (len(weights) + 2),
        out_specs=pl.BlockSpec(memory_space=pltpu.VMEM),
        compiler_params=pltpu.CompilerParams(vmem_limit_bytes=VMEM_LIMIT),
        cost_estimate=pl.CostEstimate(
            flops=2 * hidden.shape[0] * len(weights) * weights[0].size,
            bytes_accessed=2 * len(weights) * weights[0].size + 4 * hidden.size,
            transcendentals=0,
        ),
    )(attended, *weights, hidden)


def norm_kernel(latents_ref, mine_ref, theirs_ref, bias_ref, gain_ref, normed_ref, *hidden_refs):
    temporal = mine_ref[...] + theirs_ref[...].astype(jnp.float32) + bias_ref[...][None]
    hidden = latents_ref[...].astype(jnp.float32) + temporal
    hidden = hidden.astype(normed_ref.dtype)
    for hidden_ref in hidden_refs:
        hidden_ref[...] = hidden
    flat = hidden.astype(jnp.float32)
    scale = 1.0 / flat.shape[-1]
    shifted = flat - jnp.sum(flat, axis=-1, keepdims=True) * scale
    variance = jnp.sum(shifted * shifted, axis=-1, keepdims=True) * scale
    normed = shifted * (1.0 / jnp.sqrt(variance + 1e-05)) * gain_ref[...][None]
    normed_ref[...] = normed.astype(normed_ref.dtype)


def norm_of_hidden(latents, mine, theirs, bias, gain, with_hidden):
    shapes = [jax.ShapeDtypeStruct(theirs.shape, jnp.bfloat16)] * (2 if with_hidden else 1)
    return pl.pallas_call(
        norm_kernel,
        out_shape=shapes,
        in_specs=[pl.BlockSpec(memory_space=pltpu.VMEM)] * 5,
        out_specs=[pl.BlockSpec(memory_space=pltpu.VMEM)] * len(shapes),
        compiler_params=pltpu.CompilerParams(vmem_limit_bytes=VMEM_LIMIT),
        cost_estimate=pl.CostEstimate(
            flops=12 * theirs.size, bytes_accessed=12 * theirs.size, transcendentals=0
        ),
    )(latents, mine, theirs, bias, gain)


def project_kernel(*refs, pieces, frames_axis, rows_axis):
    q_ref, k_ref, v_ref, own_q, own_kv, pair_qkv, pair_kv, flat_ref, scratch = refs[pieces:]
    index = lax.axis_index(rows_axis)
    for mask, piece in enumerate(refs[:pieces]):
        flat_ref[lax.rem(index ^ mask, pieces)] = piece[...]
    flat = flat_ref[...].reshape(-1, flat_ref.shape[-1])
    _, _, share, _, tokens = scratch.shape
    for which, weight_ref in enumerate((q_ref, k_ref, v_ref)):
        product = jnp.dot(flat, weight_ref[...], preferred_element_type=jnp.float32)
        upright = product.T.astype(scratch.dtype)
        scratch[:, which] = upright.reshape(2, share, HD, tokens)
    is_odd = lax.rem(lax.axis_index(frames_axis), 2)
    own_q[...] = scratch[is_odd, 0]
    own_kv[...] = scratch[is_odd, 1:]
    pair_qkv[...] = scratch[1 - is_odd]
    pair_kv[...] = scratch[1 - is_odd, 1:]


def project(pieces, query_weight, key_weight, value_weight, frames_axis, rows_axis):
    width, channels = pieces[0].shape
    tokens = len(pieces) * width
    share = query_weight.shape[1] // HD // 2

    def shape(count):
        return jax.ShapeDtypeStruct((count, share, HD, tokens), jnp.bfloat16)

    return pl.pallas_call(
        functools.partial(
            project_kernel, pieces=len(pieces), frames_axis=frames_axis, rows_axis=rows_axis
        ),
        out_shape=[
            jax.ShapeDtypeStruct((share, HD, tokens), jnp.bfloat16),
            shape(2),
            shape(3),
            shape(2),
        ],
        in_specs=[pl.BlockSpec(memory_space=pltpu.VMEM)] * (len(pieces) + 3),
        out_specs=[pl.BlockSpec(memory_space=pltpu.VMEM)] * 4,
        scratch_shapes=[
            pltpu.VMEM((len(pieces), width, channels), jnp.bfloat16),
            pltpu.VMEM((2, 3, share, HD, tokens), jnp.bfloat16),
        ],
        compiler_params=pltpu.CompilerParams(vmem_limit_bytes=VMEM_LIMIT),
        cost_estimate=pl.CostEstimate(
            flops=6 * tokens * channels * query_weight.shape[1],
            bytes_accessed=6 * query_weight.size + 2 * tokens * channels,
            transcendentals=0,
        ),
    )(*pieces, query_weight, key_weight, value_weight)


def attention_kernel(*refs, parts, kv_count, first, last):
    own_q, kvs = refs[:parts], refs[parts : parts + kv_count]
    rest = refs[parts + kv_count :]
    pair_qkv, rest = rest[:parts], rest[parts:]
    state, outs = ((), rest) if first else (rest[:3], rest[3:])
    scale = 1.0 / math.sqrt(HD)
    contract_first = (((0,), (0,)), ((), ()))

    def wide(arrays):
        return jnp.concatenate(list(arrays), axis=1)

    for head in range(own_q[0].shape[0]):
        pairs = [(kv[0, head], kv[1, head]) for kv in kvs]
        if first:
            pairs += [(qkv[1, head], qkv[2, head]) for qkv in pair_qkv]
        groups = [pairs[i : i + parts] for i in range(0, len(pairs), parts)]
        keys = [wide(key for key, _ in group) for group in groups]
        values = [wide(value for _, value in group) for group in groups]
        asked = [q[head] for q in own_q] + [qkv[0, head] for qkv in pair_qkv]
        query = (wide(asked).astype(jnp.float32) * scale).astype(jnp.bfloat16)
        scores = [
            lax.dot_general(key, query, contract_first, preferred_element_type=jnp.float32)
            for key in keys
        ]
        peak = functools.reduce(jnp.maximum, [jnp.max(s, axis=0, keepdims=True) for s in scores])
        if first:
            denominator = jnp.zeros_like(peak)
            numerator = jnp.zeros((HD, query.shape[1]), jnp.float32)
        else:
            old_peak, denominator, numerator = (ref[head] for ref in state)
            peak = jnp.maximum(peak, old_peak)
            shrink = jnp.exp(old_peak - peak)
            denominator, numerator = denominator * shrink, numerator * shrink
        for value, score in zip(values, scores):
            weights = jnp.exp(score - peak)
            denominator = denominator + jnp.sum(weights, axis=0, keepdims=True)
            numerator = numerator + jnp.dot(
                value, weights.astype(jnp.bfloat16), preferred_element_type=jnp.float32
            )
        if last:
            result = (numerator / denominator).T
            tokens = outs[0].shape[0]
            for which, out in enumerate(outs):
                mine = result[which * tokens : (which + 1) * tokens]
                out[:, head * HD : (head + 1) * HD] = mine.astype(out.dtype)
        else:
            for ref, value in zip(outs, (peak, denominator, numerator)):
                ref[head] = value


def attend(own_q, pair_qkv, kvs, state, last):
    parts = len(own_q)
    heads, _, width = own_q[0].shape
    tokens = parts * width
    keys = (len(kvs) + (0 if state else parts)) * width
    if last:
        shapes = [jax.ShapeDtypeStruct((tokens, heads * HD), jnp.bfloat16)] * 2
    else:
        shapes = [
            jax.ShapeDtypeStruct((heads, rows, 2 * tokens), jnp.float32) for rows in (1, 1, HD)
        ]
    work = 2 * heads * tokens * keys
    args = (*own_q, *kvs, *pair_qkv, *state)
    return pl.pallas_call(
        functools.partial(
            attention_kernel, parts=parts, kv_count=len(kvs), first=not state, last=last
        ),
        out_shape=shapes,
        in_specs=[pl.BlockSpec(memory_space=pltpu.VMEM)] * len(args),
        out_specs=[pl.BlockSpec(memory_space=pltpu.VMEM)] * len(shapes),
        compiler_params=pltpu.CompilerParams(vmem_limit_bytes=VMEM_LIMIT),
        cost_estimate=pl.CostEstimate(
            flops=4 * work * HD,
            bytes_accessed=sum(a.size * a.dtype.itemsize for a in args),
            transcendentals=work,
        ),
    )(*args)


def body(
    latents,
    spatial_weight,
    spatial_bias,
    norm_gain,
    norm_shift,
    temporal_weight,
    temporal_bias,
    token_gain,
    query_weight,
    key_weight,
    value_weight,
    output_weight,
):
    rows_size, frames_size = lax.axis_size("rows"), lax.axis_size("frames")
    row_count, frame_count, width_cells, channels = latents.shape
    if rows_size != 4 or frames_size < 2 or frames_size & (frames_size - 1) or frame_count != 1:
        raise NotImplementedError("mesh shape")
    inner_size = 2
    outer_size = rows_size // inner_size
    loaded = load(jnp.swapaxes(spatial_weight, 2, 3))
    own = latents.reshape(-1, channels)
    pieces = {0: own}
    bit = rows_size // 2
    while bit > 1:
        pieces.update({m | bit: swap(piece, "rows", bit) for m, piece in pieces.items()})
        bit //= 2
    far, loaded, output_weight = lax.optimization_barrier(
        ({m: pieces[m] for m in pieces if m}, loaded, output_weight)
    )
    pieces.update(far)
    weights = {m: swap(output_weight, "rows", m) for m in (inner_size, 1)}
    weights[0] = output_weight
    pieces.update({m | 1: swap(piece, "rows", 1) for m, piece in pieces.items()})
    pieces = [pieces[m] for m in range(rows_size)]
    local_out = spatial_weight.shape[3]
    activated = conv_norm(
        pieces,
        *loaded,
        spatial_bias,
        norm_gain,
        norm_shift,
        width_cells,
        NORM_GROUPS // rows_size,
        "rows",
    )
    first, second = neighbours(activated, "frames")
    send, chip_sum = spread(
        [activated, first, second],
        ((1, 1), (2, 0), (0, 2)),
        temporal_weight.reshape(3 * local_out, channels),
        outer_size,
        ("frames",),
        "rows",
    )
    sends, keeps = merge(chip_sum, swap(send, "rows", 1), "rows", inner_size)
    sends, weights = lax.optimization_barrier((sends, weights))
    others = [swap(sends[1 - mask], "rows", inner_size) for mask in range(outer_size)]
    tokens = []
    for mask in range(outer_size):
        normed, *wanted = norm_of_hidden(
            pieces[mask * inner_size],
            keeps[mask],
            others[mask],
            temporal_bias,
            token_gain,
            mask == 0,
        )
        hidden = wanted[0] if wanted else hidden
        tokens.append([normed, swap(normed, "rows", 1)])
        tokens[0], others = lax.optimization_barrier((tokens[0], others))
    own_q, own_kv, pair_qkv, far = [], [], [], []
    for mask in range(outer_size):
        q, kv, *sent = project(
            tokens[mask], query_weight, key_weight, value_weight, "frames", "rows"
        )
        own_q.append(q)
        own_kv.append(kv)
        far.append(
            [
                swap(sent[1] if m % 2 else kv, "frames", m)
                for m in range(2, frames_size)
            ]
        )
        pair_qkv.append(swap(sent[0], "frames", 1))
    early, late = own_kv + far[0][:1], far[0][1:] + far[1]
    state = attend(own_q, pair_qkv, early, (), not late)
    own_out, pair_out = attend(own_q, pair_qkv, late, state, True) if late else state
    own_out, pair_out, weights = lax.optimization_barrier((own_out, pair_out, weights))
    weights[inner_size + 1] = swap(weights[inner_size], "rows", 1)
    dealt = deal(own_out, pair_out, rows_size, "frames", "rows", inner_size)
    together = 2 * rows_size
    groups = [
        list(range(start, start + together))
        for start in range(0, frames_size * rows_size, together)
    ]
    arrived = lax.all_to_all(
        dealt.reshape((together,) + dealt.shape[2:]),
        ("frames", "rows"),
        0,
        0,
        axis_index_groups=groups,
        tiled=True,
    )
    weights = [weights[m] for m in range(rows_size)]
    result = finish(arrived.reshape(dealt.shape), weights, hidden, "rows")
    return result.reshape(latents.shape)


def solution(mesh):
    in_specs = (
        P("rows", ("groups", "frames"), None, None),
        P(None, None, None, "rows"),
        P("rows"),
        P("rows"),
        P("rows"),
        P(None, "rows", None),
        P(),
        P(),
        P(None, "rows"),
        P(None, "rows"),
        P(None, "rows"),
        P("rows", None),
    )
    out_specs = P("rows", ("groups", "frames"), None, None)
    return jax.shard_map(body, mesh=mesh, in_specs=in_specs, out_specs=out_specs, check_vma=False)
```

```python
import functools
import math

import jax
import jax.numpy as jnp
from jax import lax
from jax.experimental import pallas as pl
from jax.experimental.pallas import tpu as pltpu
from jax.sharding import PartitionSpec as P

HD = 64
NORM_GROUPS = 32
VMEM_LIMIT = 16 * 1024 * 1024


def swap(array, axis, stride):
    size = lax.axis_size(axis)
    return lax.ppermute(array, axis, [(i, i ^ stride) for i in range(size)])


def neighbours(array, axis):
    size = lax.axis_size(axis)
    even = [(i, i ^ 1) for i in range(size) if i ^ 1 < size]
    odd = [(i, ((i + 1) ^ 1) - 1) for i in range(1, size) if ((i + 1) ^ 1) - 1 < size]
    return lax.ppermute(array, axis, even), lax.ppermute(array, axis, odd)


def load_kernel(*refs):
    half = len(refs) // 2
    sems = refs[-1]
    copies = [
        pltpu.make_async_copy(source, target, sems.at[i])
        for i, (source, target) in enumerate(zip(refs[:half], refs[half : 2 * half]))
    ]
    for copy in copies:
        copy.start()
    for copy in copies:
        copy.wait()


def load(*arrays):
    return pl.pallas_call(
        load_kernel,
        out_shape=[jax.ShapeDtypeStruct(a.shape, a.dtype) for a in arrays],
        in_specs=[pl.BlockSpec(memory_space=pltpu.HBM)] * len(arrays),
        out_specs=[pl.BlockSpec(memory_space=pltpu.VMEM)] * len(arrays),
        scratch_shapes=[pltpu.SemaphoreType.DMA((len(arrays),))],
        compiler_params=pltpu.CompilerParams(vmem_limit_bytes=VMEM_LIMIT),
        cost_estimate=pl.CostEstimate(
            flops=0, bytes_accessed=sum(a.size * a.dtype.itemsize for a in arrays), transcendentals=0
        ),
    )(*arrays)


def conv_kernel(*refs, pieces, cols, groups, axis):
    plane_refs = refs[:pieces]
    weight_ref, bias_ref, gain_ref, shift_ref, out_ref, padded_ref = refs[pieces:]
    share, chans = plane_refs[0].shape
    tokens = pieces * share
    outs = out_ref.shape[0]
    padded_ref[0:cols] = jnp.zeros((cols, chans), padded_ref.dtype)
    padded_ref[cols + tokens : tokens + 2 * cols] = jnp.zeros((cols, chans), padded_ref.dtype)
    index = lax.axis_index(axis)
    for mask, piece in enumerate(plane_refs):
        start = pl.multiple_of((index ^ mask) * share + cols, math.gcd(share, cols))
        padded_ref[pl.ds(start, share)] = piece[...]
    total = None
    for row_off in range(3):
        window = padded_ref[row_off * cols : row_off * cols + tokens]
        weight = weight_ref[row_off].reshape(3 * outs, chans)
        term = lax.dot_general(
            weight, window, (((1,), (1,)), ((), ())), preferred_element_type=jnp.float32
        )
        total = term if total is None else total + term
    column = lax.broadcasted_iota(jnp.int32, (outs, tokens), 1) % cols
    left = jnp.where(column == 0, 0.0, pltpu.roll(total[:outs], 1, 1))
    right = jnp.where(column == cols - 1, 0.0, pltpu.roll(total[2 * outs :], tokens - 1, 1))

    diagonal = lax.broadcasted_iota(jnp.int32, (outs, outs), 0) == lax.broadcasted_iota(
        jnp.int32, (outs, outs), 1
    )

    def upright(row):
        return jnp.sum(jnp.where(diagonal, row[None], 0.0), axis=1, keepdims=True)

    spatial = total[outs : 2 * outs] + left + right + upright(bias_ref[...])
    per_group = outs // groups
    count = per_group * tokens

    def group_mean(values):
        sums = jnp.sum(values, axis=1, keepdims=True).reshape(groups, per_group, 1)
        sums = jnp.sum(sums, axis=1, keepdims=True) * (1.0 / count)
        return jnp.broadcast_to(sums, (groups, per_group, 1)).reshape(outs, 1)

    centred = spatial - group_mean(spatial)
    inverse = 1.0 / jnp.sqrt(group_mean(centred * centred) + 1e-05)
    scaled = centred * (inverse * upright(gain_ref[...])) + upright(shift_ref[...])
    out_ref[...] = (scaled / (1.0 + jnp.exp(-scaled))).astype(out_ref.dtype)


def conv_norm(pieces, weight, bias, gain, shift, cols, groups, rows_axis):
    share, chans = pieces[0].shape
    tokens, outs = share * len(pieces), weight.shape[2]
    return pl.pallas_call(
        functools.partial(
            conv_kernel, pieces=len(pieces), cols=cols, groups=groups, axis=rows_axis
        ),
        out_shape=jax.ShapeDtypeStruct((outs, tokens), jnp.bfloat16),
        in_specs=[pl.BlockSpec(memory_space=pltpu.VMEM)] * (len(pieces) + 4),
        out_specs=pl.BlockSpec(memory_space=pltpu.VMEM),
        scratch_shapes=[pltpu.VMEM((tokens + 2 * cols, chans), jnp.bfloat16)],
        compiler_params=pltpu.CompilerParams(vmem_limit_bytes=VMEM_LIMIT),
        cost_estimate=pl.CostEstimate(
            flops=18 * tokens * outs * chans,
            bytes_accessed=2 * (weight.size + tokens * chans + outs * tokens),
            transcendentals=outs * tokens,
        ),
    )(*pieces, weight, bias, gain, shift)


def spread_kernel(*refs, places, parity_axes, rows_axis):
    pieces = refs[: len(places)]
    weight_ref, send_ref, rest_ref, stack_ref, rows_ref = refs[len(places) :]
    k = pieces[0].shape[0]
    outer_count, width, _ = rest_ref.shape
    inner_count = rows_ref.shape[0] // outer_count
    is_odd = lax.rem(sum(lax.axis_index(axis) for axis in parity_axes), 2)
    for piece, (even, odd) in zip(pieces, places):
        start = even * k if even == odd else pl.multiple_of((even + is_odd * (odd - even)) * k, 16)
        stack_ref[pl.ds(start, k)] = piece[...]
    rows_ref[...] = stack_ref[...].T.reshape(rows_ref.shape)
    mine = lax.rem(lax.axis_index(rows_axis), inner_count)
    sent = [rows_ref[outer * inner_count + 1 - mine] for outer in range(outer_count)]
    product = jnp.dot(
        jnp.concatenate(sent, axis=0), weight_ref[...], preferred_element_type=jnp.float32
    )
    send_ref[...] = product.astype(send_ref.dtype).reshape(send_ref.shape)
    for outer in range(outer_count):
        rest_ref[outer] = rows_ref[outer * inner_count + mine]


def keep_kernel(rest_ref, weight_ref, keep_ref):
    rest = rest_ref[...].reshape(-1, rest_ref.shape[-1])
    product = jnp.dot(rest, weight_ref[...], preferred_element_type=jnp.float32)
    keep_ref[...] = product.reshape(keep_ref.shape)


def spread(pieces, places, weight, outer_count, parity_axes, rows_axis):
    k, tokens = pieces[0].shape
    depth, channels = weight.shape
    width = tokens // (2 * outer_count)
    part = (outer_count, width, channels)
    estimate = pl.CostEstimate(
        flops=tokens * depth * channels,
        bytes_accessed=2 * weight.size + 3 * tokens * channels,
        transcendentals=0,
    )
    send, rest = pl.pallas_call(
        functools.partial(
            spread_kernel, places=places, parity_axes=parity_axes, rows_axis=rows_axis
        ),
        out_shape=[
            jax.ShapeDtypeStruct(part, jnp.bfloat16),
            jax.ShapeDtypeStruct((outer_count, width, depth), jnp.bfloat16),
        ],
        in_specs=[pl.BlockSpec(memory_space=pltpu.VMEM)] * (len(pieces) + 1),
        out_specs=[pl.BlockSpec(memory_space=pltpu.VMEM)] * 2,
        scratch_shapes=[
            pltpu.VMEM((depth, tokens), jnp.bfloat16),
            pltpu.VMEM((2 * outer_count, width, depth), jnp.bfloat16),
        ],
        compiler_params=pltpu.CompilerParams(vmem_limit_bytes=VMEM_LIMIT),
        cost_estimate=estimate,
    )(*pieces, weight)
    keep = pl.pallas_call(
        keep_kernel,
        out_shape=jax.ShapeDtypeStruct(part, jnp.float32),
        in_specs=[pl.BlockSpec(memory_space=pltpu.VMEM)] * 2,
        out_specs=pl.BlockSpec(memory_space=pltpu.VMEM),
        compiler_params=pltpu.CompilerParams(vmem_limit_bytes=VMEM_LIMIT),
        cost_estimate=estimate,
    )(rest, weight)
    return send, keep


def merge_kernel(mine_ref, theirs_ref, *refs, axis, inner_count):
    place = lax.div(lax.axis_index(axis), inner_count)
    for mask, (send_ref, keep_ref) in enumerate(zip(refs[::2], refs[1::2])):
        total = mine_ref[place ^ mask] + theirs_ref[place ^ mask].astype(jnp.float32)
        send_ref[...] = total.astype(send_ref.dtype)
        keep_ref[...] = total


def merge(mine, theirs, rows_axis, inner_count):
    shapes = [
        jax.ShapeDtypeStruct(theirs.shape[1:], dtype) for dtype in (jnp.bfloat16, jnp.float32)
    ] * theirs.shape[0]
    outs = pl.pallas_call(
        functools.partial(merge_kernel, axis=rows_axis, inner_count=inner_count),
        out_shape=shapes,
        in_specs=[pl.BlockSpec(memory_space=pltpu.VMEM)] * 2,
        out_specs=[pl.BlockSpec(memory_space=pltpu.VMEM)] * len(shapes),
        compiler_params=pltpu.CompilerParams(vmem_limit_bytes=VMEM_LIMIT),
        cost_estimate=pl.CostEstimate(
            flops=theirs.size, bytes_accessed=12 * theirs.size, transcendentals=0
        ),
    )(mine, theirs)
    return outs[::2], outs[1::2]


def deal_kernel(own_ref, pair_ref, out_ref, *, frames_axis, rows_axis, inner_count):
    _, rows, width, _ = out_ref.shape
    is_odd = lax.rem(lax.axis_index(frames_axis), 2)
    index = lax.axis_index(rows_axis)
    for source, frame in ((own_ref, is_odd), (pair_ref, 1 - is_odd)):
        for mask in range(rows):
            place = mask // inner_count * inner_count + lax.rem(index ^ mask, inner_count)
            start = pl.multiple_of(place * width, width)
            out_ref[frame, index ^ mask] = source[pl.ds(start, width)]


def deal(own, pair, rows, frames_axis, rows_axis, inner_count):
    tokens, columns = own.shape
    return pl.pallas_call(
        functools.partial(
            deal_kernel, frames_axis=frames_axis, rows_axis=rows_axis, inner_count=inner_count
        ),
        out_shape=jax.ShapeDtypeStruct((2, rows, tokens // rows, columns), jnp.bfloat16),
        in_specs=[pl.BlockSpec(memory_space=pltpu.VMEM)] * 2,
        out_specs=pl.BlockSpec(memory_space=pltpu.VMEM),
        compiler_params=pltpu.CompilerParams(vmem_limit_bytes=VMEM_LIMIT),
        cost_estimate=pl.CostEstimate(
            flops=0, bytes_accessed=8 * tokens * columns, transcendentals=0
        ),
    )(own, pair)


def finish_kernel(attended_ref, *refs, axis):
    weights, (hidden_ref, out_ref) = refs[:-2], refs[-2:]
    index = lax.axis_index(axis)
    total = hidden_ref[...].astype(jnp.float32)
    for mask, weight in enumerate(weights):
        halves = [attended_ref[frame, index ^ mask] for frame in range(2)]
        columns = jnp.concatenate(halves, axis=1)
        total = total + jnp.dot(columns, weight[...], preferred_element_type=jnp.float32)
    out_ref[...] = total.astype(out_ref.dtype)


def finish(attended, weights, hidden, rows_axis):
    return pl.pallas_call(
        functools.partial(finish_kernel, axis=rows_axis),
        out_shape=jax.ShapeDtypeStruct(hidden.shape, hidden.dtype),
        in_specs=[pl.BlockSpec(memory_space=pltpu.VMEM)] * (len(weights) + 2),
        out_specs=pl.BlockSpec(memory_space=pltpu.VMEM),
        compiler_params=pltpu.CompilerParams(vmem_limit_bytes=VMEM_LIMIT),
        cost_estimate=pl.CostEstimate(
            flops=2 * hidden.shape[0] * len(weights) * weights[0].size,
            bytes_accessed=2 * len(weights) * weights[0].size + 4 * hidden.size,
            transcendentals=0,
        ),
    )(attended, *weights, hidden)


def norm_kernel(latents_ref, mine_ref, theirs_ref, bias_ref, gain_ref, normed_ref, *hidden_refs):
    temporal = mine_ref[...] + theirs_ref[...].astype(jnp.float32) + bias_ref[...][None]
    hidden = latents_ref[...].astype(jnp.float32) + temporal
    hidden = hidden.astype(normed_ref.dtype)
    for hidden_ref in hidden_refs:
        hidden_ref[...] = hidden
    flat = hidden.astype(jnp.float32)
    scale = 1.0 / flat.shape[-1]
    shifted = flat - jnp.sum(flat, axis=-1, keepdims=True) * scale
    variance = jnp.sum(shifted * shifted, axis=-1, keepdims=True) * scale
    normed = shifted * (1.0 / jnp.sqrt(variance + 1e-05)) * gain_ref[...][None]
    normed_ref[...] = normed.astype(normed_ref.dtype)


def norm_of_hidden(latents, mine, theirs, bias, gain, with_hidden):
    shapes = [jax.ShapeDtypeStruct(theirs.shape, jnp.bfloat16)] * (2 if with_hidden else 1)
    return pl.pallas_call(
        norm_kernel,
        out_shape=shapes,
        in_specs=[pl.BlockSpec(memory_space=pltpu.VMEM)] * 5,
        out_specs=[pl.BlockSpec(memory_space=pltpu.VMEM)] * len(shapes),
        compiler_params=pltpu.CompilerParams(vmem_limit_bytes=VMEM_LIMIT),
        cost_estimate=pl.CostEstimate(
            flops=12 * theirs.size, bytes_accessed=12 * theirs.size, transcendentals=0
        ),
    )(latents, mine, theirs, bias, gain)


def project_kernel(*refs, pieces, frames_axis, rows_axis):
    q_ref, k_ref, v_ref, own_q, own_kv, pair_qkv, pair_kv, flat_ref, scratch = refs[pieces:]
    index = lax.axis_index(rows_axis)
    for mask, piece in enumerate(refs[:pieces]):
        flat_ref[lax.rem(index ^ mask, pieces)] = piece[...]
    flat = flat_ref[...].reshape(-1, flat_ref.shape[-1])
    _, _, share, _, tokens = scratch.shape
    for which, weight_ref in enumerate((q_ref, k_ref, v_ref)):
        product = jnp.dot(flat, weight_ref[...], preferred_element_type=jnp.float32)
        upright = product.T.astype(scratch.dtype)
        scratch[:, which] = upright.reshape(2, share, HD, tokens)
    is_odd = lax.rem(lax.axis_index(frames_axis), 2)
    own_q[...] = scratch[is_odd, 0]
    own_kv[...] = scratch[is_odd, 1:]
    pair_qkv[...] = scratch[1 - is_odd]
    pair_kv[...] = scratch[1 - is_odd, 1:]


def project(pieces, query_weight, key_weight, value_weight, frames_axis, rows_axis):
    width, channels = pieces[0].shape
    tokens = len(pieces) * width
    share = query_weight.shape[1] // HD // 2

    def shape(count):
        return jax.ShapeDtypeStruct((count, share, HD, tokens), jnp.bfloat16)

    return pl.pallas_call(
        functools.partial(
            project_kernel, pieces=len(pieces), frames_axis=frames_axis, rows_axis=rows_axis
        ),
        out_shape=[
            jax.ShapeDtypeStruct((share, HD, tokens), jnp.bfloat16),
            shape(2),
            shape(3),
            shape(2),
        ],
        in_specs=[pl.BlockSpec(memory_space=pltpu.VMEM)] * (len(pieces) + 3),
        out_specs=[pl.BlockSpec(memory_space=pltpu.VMEM)] * 4,
        scratch_shapes=[
            pltpu.VMEM((len(pieces), width, channels), jnp.bfloat16),
            pltpu.VMEM((2, 3, share, HD, tokens), jnp.bfloat16),
        ],
        compiler_params=pltpu.CompilerParams(vmem_limit_bytes=VMEM_LIMIT),
        cost_estimate=pl.CostEstimate(
            flops=6 * tokens * channels * query_weight.shape[1],
            bytes_accessed=6 * query_weight.size + 2 * tokens * channels,
            transcendentals=0,
        ),
    )(*pieces, query_weight, key_weight, value_weight)


def attention_kernel(*refs, parts, kv_count, first, last):
    own_q, kvs = refs[:parts], refs[parts : parts + kv_count]
    rest = refs[parts + kv_count :]
    pair_qkv, rest = rest[:parts], rest[parts:]
    state, outs = ((), rest) if first else (rest[:3], rest[3:])
    scale = 1.0 / math.sqrt(HD)
    contract_first = (((0,), (0,)), ((), ()))

    def wide(arrays):
        return jnp.concatenate(list(arrays), axis=1)

    for head in range(own_q[0].shape[0]):
        pairs = [(kv[0, head], kv[1, head]) for kv in kvs]
        if first:
            pairs += [(qkv[1, head], qkv[2, head]) for qkv in pair_qkv]
        groups = [pairs[i : i + parts] for i in range(0, len(pairs), parts)]
        keys = [wide(key for key, _ in group) for group in groups]
        values = [wide(value for _, value in group) for group in groups]
        asked = [q[head] for q in own_q] + [qkv[0, head] for qkv in pair_qkv]
        query = (wide(asked).astype(jnp.float32) * scale).astype(jnp.bfloat16)
        scores = [
            lax.dot_general(key, query, contract_first, preferred_element_type=jnp.float32)
            for key in keys
        ]
        peak = functools.reduce(jnp.maximum, [jnp.max(s, axis=0, keepdims=True) for s in scores])
        if first:
            denominator = jnp.zeros_like(peak)
            numerator = jnp.zeros((HD, query.shape[1]), jnp.float32)
        else:
            old_peak, denominator, numerator = (ref[head] for ref in state)
            peak = jnp.maximum(peak, old_peak)
            shrink = jnp.exp(old_peak - peak)
            denominator, numerator = denominator * shrink, numerator * shrink
        for value, score in zip(values, scores):
            weights = jnp.exp(score - peak)
            denominator = denominator + jnp.sum(weights, axis=0, keepdims=True)
            numerator = numerator + jnp.dot(
                value, weights.astype(jnp.bfloat16), preferred_element_type=jnp.float32
            )
        if last:
            result = (numerator / denominator).T
            tokens = outs[0].shape[0]
            for which, out in enumerate(outs):
                mine = result[which * tokens : (which + 1) * tokens]
                out[:, head * HD : (head + 1) * HD] = mine.astype(out.dtype)
        else:
            for ref, value in zip(outs, (peak, denominator, numerator)):
                ref[head] = value


def attend(own_q, pair_qkv, kvs, state, last):
    parts = len(own_q)
    heads, _, width = own_q[0].shape
    tokens = parts * width
    keys = (len(kvs) + (0 if state else parts)) * width
    if last:
        shapes = [jax.ShapeDtypeStruct((tokens, heads * HD), jnp.bfloat16)] * 2
    else:
        shapes = [
            jax.ShapeDtypeStruct((heads, rows, 2 * tokens), jnp.float32) for rows in (1, 1, HD)
        ]
    work = 2 * heads * tokens * keys
    args = (*own_q, *kvs, *pair_qkv, *state)
    return pl.pallas_call(
        functools.partial(
            attention_kernel, parts=parts, kv_count=len(kvs), first=not state, last=last
        ),
        out_shape=shapes,
        in_specs=[pl.BlockSpec(memory_space=pltpu.VMEM)] * len(args),
        out_specs=[pl.BlockSpec(memory_space=pltpu.VMEM)] * len(shapes),
        compiler_params=pltpu.CompilerParams(vmem_limit_bytes=VMEM_LIMIT),
        cost_estimate=pl.CostEstimate(
            flops=4 * work * HD,
            bytes_accessed=sum(a.size * a.dtype.itemsize for a in args),
            transcendentals=work,
        ),
    )(*args)


def body(
    latents,
    spatial_weight,
    spatial_bias,
    norm_gain,
    norm_shift,
    temporal_weight,
    temporal_bias,
    token_gain,
    query_weight,
    key_weight,
    value_weight,
    output_weight,
):
    rows_size, frames_size = lax.axis_size("rows"), lax.axis_size("frames")
    row_count, frame_count, width_cells, channels = latents.shape
    if rows_size != 4 or frames_size < 2 or frames_size & (frames_size - 1) or frame_count != 1:
        raise NotImplementedError("mesh shape")
    inner_size = 2
    outer_size = rows_size // inner_size
    loaded = load(jnp.swapaxes(spatial_weight, 2, 3))
    own = latents.reshape(-1, channels)
    pieces = {0: own}
    bit = rows_size // 2
    while bit > 1:
        pieces.update({m | bit: swap(piece, "rows", bit) for m, piece in pieces.items()})
        bit //= 2
    far, loaded, output_weight = lax.optimization_barrier(
        ({m: pieces[m] for m in pieces if m}, loaded, output_weight)
    )
    pieces.update(far)
    weights = {0: output_weight, inner_size: swap(output_weight, "rows", inner_size)}
    pieces.update({m | 1: swap(piece, "rows", 1) for m, piece in pieces.items()})
    pieces = [pieces[m] for m in range(rows_size)]
    local_out = spatial_weight.shape[3]
    activated = conv_norm(
        pieces,
        *loaded,
        spatial_bias,
        norm_gain,
        norm_shift,
        width_cells,
        NORM_GROUPS // rows_size,
        "rows",
    )
    first, second = neighbours(activated, "frames")
    send, chip_sum = spread(
        [activated, second, first],
        ((1, 1), (0, 2), (2, 0)),
        temporal_weight.reshape(3 * local_out, channels),
        outer_size,
        ("frames",),
        "rows",
    )
    sends, keeps = merge(chip_sum, swap(send, "rows", 1), "rows", inner_size)
    sends, weights = lax.optimization_barrier((sends, weights))
    others = [swap(sends[1 - mask], "rows", inner_size) for mask in range(outer_size)]
    tokens = []
    for mask in range(outer_size):
        normed, *wanted = norm_of_hidden(
            pieces[mask * inner_size],
            keeps[mask],
            others[mask],
            temporal_bias,
            token_gain,
            mask == 0,
        )
        hidden = wanted[0] if wanted else hidden
        tokens.append([normed, swap(normed, "rows", 1)])
        tokens[0], others = lax.optimization_barrier((tokens[0], others))
    own_q, own_kv, pair_qkv, far = [], [], [], []
    for mask in range(outer_size):
        q, kv, *sent = project(
            tokens[mask], query_weight, key_weight, value_weight, "frames", "rows"
        )
        own_q.append(q)
        own_kv.append(kv)
        far.append(
            [
                swap(sent[1] if m % 2 else kv, "frames", m)
                for m in range(2, frames_size)
            ]
        )
        pair_qkv.append(swap(sent[0], "frames", 1))
    turns = [own_kv + far[0][:1], far[0][1:] + far[1][1:], far[1][:1]]
    turns = [kvs for kvs in turns if kvs]
    state = ()
    for turn, kvs in enumerate(turns):
        state = attend(own_q, pair_qkv, kvs, state, turn == len(turns) - 1)
    own_out, pair_out = state
    own_out, pair_out, weights = lax.optimization_barrier((own_out, pair_out, weights))
    weights.update({m | 1: swap(weight, "rows", 1) for m, weight in weights.items()})
    dealt = deal(own_out, pair_out, rows_size, "frames", "rows", inner_size)
    together = 2 * rows_size
    groups = [
        list(range(start, start + together))
        for start in range(0, frames_size * rows_size, together)
    ]
    arrived = lax.all_to_all(
        dealt.reshape((together,) + dealt.shape[2:]),
        ("frames", "rows"),
        0,
        0,
        axis_index_groups=groups,
        tiled=True,
    )
    weights = [weights[m] for m in range(rows_size)]
    result = finish(arrived.reshape(dealt.shape), weights, hidden, "rows")
    return result.reshape(latents.shape)


def solution(mesh):
    in_specs = (
        P("rows", ("groups", "frames"), None, None),
        P(None, None, None, "rows"),
        P("rows"),
        P("rows"),
        P("rows"),
        P(None, "rows", None),
        P(),
        P(),
        P(None, "rows"),
        P(None, "rows"),
        P(None, "rows"),
        P("rows", None),
    )
    out_specs = P("rows", ("groups", "frames"), None, None)
    return jax.shard_map(body, mesh=mesh, in_specs=in_specs, out_specs=out_specs, check_vma=False)
```
